128 devices in a mesh: front: 16 (over z, y), blk: 8 (over x, core).
Axes of the slice: x: 4, y: 4, z: 4, core: 2. Of those that a mesh axis runs over, the one named last changes fastest.
Arguments:
- contribution: bfloat16 [16, 8192, 8192], P('front', 'blk'), may hold values from -0.0625 to 0.0625
- omega_cols: bfloat16 [16, 8192, 256], P('front', 'blk'), may hold values from -6 to 6
- psi_cols: bfloat16 [16, 8192, 256], P('front', 'blk'), may hold values from -6 to 6
- lengths: int32 [16], P('front'), may hold values from 1024 to 8192, as said below
- selectors: int32 [16, 64], P('front', 'blk'), may hold values from 0 to 15, as said below
- assign: int32 [16, 1], replicated, may hold values from 0 to 3
- pivot_block: float32 [4, 256, 256], replicated, as said below
Outputs:
- row_panel: float32 [8, 2048, 4, 256], P('blk', 'front')
- col_panel: float32 [8, 2048, 4, 256], P('blk', 'front')
The draws below stay inside these ranges and needn't reach their ends.
Inputs may be any that keep to these rules, and one draw needn't show every extreme that they name: `lengths`: the largest length equals 8192. `selectors`: for one child and one row block the values are distinct. `assign`: every parent has at least one child. `pivot_block`: symmetric, each diagonal entry exceeds the sum of magnitudes of the rest of its row.
All inputs are finite; a program needn't handle non-finite values.
Results may differ from the reference program's by a relative error of at most 0.0003.
Values may be sent and summed in bfloat16 or wider, within the bound.
A program may use at most 128 MiB of HBM per device.

```python
import jax
import jax.numpy as jnp
from jax import lax

NC = 8192
R = 256
SB = 128
CHILDREN = 16
PARENTS = 4
NPR = 16384
N_BLK = 8


def draw_lengths(key, part):
    key = jax.random.fold_in(key, 11)
    first_key, second_key = jax.random.split(key)
    values = jax.random.randint(first_key, (CHILDREN,), NC // 8, NC + 1)
    position = jax.random.randint(second_key, (), 0, CHILDREN)
    return jnp.where(jnp.arange(CHILDREN) == position, NC, values).astype(jnp.int32)


def draw_selectors(key, part):
    key = jax.random.fold_in(key, 23)
    sub_count = NC // (SB * N_BLK)
    scores = jax.random.randint(key, (CHILDREN, N_BLK, 2 * sub_count), 0, 1 << 20)
    scores = scores * (2 * sub_count) + jnp.arange(2 * sub_count, dtype=jnp.int32)
    ordering = jnp.argsort(scores, axis=-1, stable=True)
    return ordering[:, :, :sub_count].reshape(CHILDREN, NC // SB).astype(jnp.int32)


def draw_pivot_block(key, part):
    key = jax.random.fold_in(key, 37)
    first_key, second_key = jax.random.split(key)
    raw_entries = jax.random.uniform(first_key, (PARENTS, R, R), jnp.float32, -1.0, 1.0) / R
    diagonal = jax.random.uniform(second_key, (PARENTS, R), jnp.float32, 1.0, 2.0)
    symmetric = (raw_entries + jnp.transpose(raw_entries, (0, 2, 1))) * 0.5
    identity = jnp.eye(R, dtype=jnp.float32)
    return symmetric * (1.0 - identity) + diagonal[:, :, None] * identity


def level_of(rng, shape, cuts, least, high):
    def one(dim, parts):
        steps = jax.random.uniform(jax.random.fold_in(jax.random.fold_in(rng, 6), dim), (parts,), jnp.float32, least / len(cuts), high / len(cuts))
        return jnp.repeat(jnp.exp(steps), shape[dim] // parts).reshape((-1,) + (1,) * (len(shape) - dim - 1))

    level = one(*cuts[0])
    for cut in cuts[1:]:
        level = level * one(*cut)
    return level


def picks_of(stream_key, rows, amount, top, lift):
    order = jax.random.permutation(jax.random.fold_in(stream_key, 1), amount)
    pull = order
    for power in range(3):
        pull = pull * pull // amount
    pull = pull * lift // amount
    chance = jax.random.randint(jax.random.fold_in(stream_key, 2), (rows, amount), 0, 4096) + pull
    sure = jax.random.permutation(jax.random.fold_in(stream_key, 3), rows)[jnp.arange(amount) % rows]
    chance = jnp.where(jnp.arange(rows)[:, None] == sure[None, :], 1 << 14, chance)
    score = chance * amount + jnp.arange(amount)
    return lax.top_k(score.astype(jnp.int32), top)[1].astype(jnp.int32)


def noise(own_key, dims, spread, limit, cuts=(), kind=jnp.bfloat16):
    gain = level_of(own_key, dims, cuts, -0.22, 0.18) if cuts else 1.0
    result = jax.random.normal(own_key, dims, jnp.float32) * spread * gain
    return jnp.minimum(jnp.maximum(result, -limit), limit).astype(kind)


def setup_inputs(seed: int = 0) -> dict:
    streams_of = jax.random.split(jax.random.key(seed), 8)
    return {
        "contribution": noise(streams_of[0], (CHILDREN, NC, NC), NC ** -0.5, 0.0625, ((0, 16), (1, 8))),
        "omega_cols": noise(streams_of[1], (CHILDREN, NC, R), 1.0, 6.0, ((0, 16), (1, 8))),
        "psi_cols": noise(streams_of[2], (CHILDREN, NC, R), 1.0, 6.0, ((0, 16), (1, 8))),
        "lengths": draw_lengths(jax.random.fold_in(streams_of[7], 71), 0),
        "selectors": draw_selectors(jax.random.fold_in(streams_of[7], 71), 0),
        "assign": picks_of(streams_of[5], CHILDREN, PARENTS, 1, 4096),
        "pivot_block": draw_pivot_block(jax.random.fold_in(streams_of[7], 71), 0),
    }


def extend_rows(samples, chosen):
    sub_count = chosen.shape[0]
    sub_blocks = samples.reshape(2, sub_count, -1, samples.shape[-1])
    parent_slots = jnp.arange(2 * sub_count, dtype=jnp.int32)
    onehot = (chosen[None, :] == parent_slots[:, None]).astype(samples.dtype)
    extended = jnp.einsum('mk,tksr->tmsr', onehot, sub_blocks, precision=lax.Precision.HIGHEST)
    return extended.reshape(2, -1, samples.shape[-1])

def panel_solve(factor, sample_rows):
    return jax.scipy.linalg.solve_triangular(factor, sample_rows.T, lower=True).T

def reference(contribution, omega_cols, psi_cols, lengths, selectors, assign, pivot_block):
    all_rows = jnp.arange(NC, dtype=jnp.int32)
    parent_ids = jnp.arange(PARENTS, dtype=jnp.int32)

    def one_child(accumulated, child_args):
        front_block, omega_local, psi_local, length, chosen, parent = child_args
        live_rows = all_rows < length
        omega_live = jnp.where(live_rows[:, None], omega_local, jnp.zeros_like(omega_local))
        psi_live = jnp.where(live_rows[:, None], psi_local, jnp.zeros_like(psi_local))
        row_sample = jnp.dot(front_block.astype(jnp.float32), omega_live.astype(jnp.float32), preferred_element_type=jnp.float32)
        col_sample = lax.dot_general(front_block.astype(jnp.float32), psi_live.astype(jnp.float32), (((0,), (0,)), ((), ())), preferred_element_type=jnp.float32)
        stacked = jnp.stack([row_sample, col_sample])
        stacked = jnp.where(live_rows[None, :, None], stacked, jnp.zeros_like(stacked))
        by_block = stacked.reshape(2, N_BLK, NC // N_BLK, R)
        chosen_blocks = chosen.reshape(N_BLK, -1)
        extended = jax.vmap(extend_rows, in_axes=(1, 0), out_axes=1)(by_block, chosen_blocks)
        extended = extended.reshape(2, NPR, R)
        parent_pick = (parent[0] == parent_ids).astype(jnp.float32)
        accumulated = accumulated + jnp.einsum('tnr,p->tnpr', extended, parent_pick, precision=lax.Precision.HIGHEST)
        return (accumulated, None)
    start_sum = jnp.zeros((2, NPR, PARENTS, R), jnp.float32)
    summed, _ = lax.scan(one_child, start_sum, (contribution, omega_cols, psi_cols, lengths, selectors, assign))
    factor = jnp.linalg.cholesky(pivot_block)
    row_solved = jax.vmap(panel_solve, in_axes=(0, 1), out_axes=1)(factor, summed[0])
    col_solved = jax.vmap(panel_solve, in_axes=(0, 1), out_axes=1)(factor, summed[1])
    row_panel = row_solved.reshape(N_BLK, NPR // N_BLK, PARENTS, R)
    col_panel = col_solved.reshape(N_BLK, NPR // N_BLK, PARENTS, R)
    return (row_panel, col_panel)
```

```python
import functools

import jax
import jax.numpy as jnp
from jax import lax
from jax.experimental import pallas as pl
from jax.experimental.pallas import tpu as pltpu
from jax.sharding import PartitionSpec as P

MESH = pl.DeviceIdType.MESH
HI = lax.Precision.HIGHEST
F32 = jnp.float32
I32 = jnp.int32
BF16 = jnp.bfloat16
NB = 64
TOP = 32766.0


def join16(t, axis):
    half = t.shape[axis] // 2
    low = lax.slice_in_dim(t, 0, half, axis=axis)
    high = lax.slice_in_dim(t, half, 2 * half, axis=axis)
    return (high << 16) | (low & 0xFFFF)


def scale_of(v):
    m = jnp.max(jnp.abs(v), axis=0, keepdims=True)
    e = jnp.floor(jnp.log2(jnp.maximum(m, 2.0**-100))) + 1.0
    return e, jnp.exp2(-e) * TOP


def encode_lanes(v):
    e, factor = scale_of(v)
    q = jnp.round(v * factor).astype(I32)
    ex = join16(e.astype(I32), 1)
    return join16(q, 1), jnp.broadcast_to(ex, (8, ex.shape[1]))


def encode_rows(v):
    e, factor = scale_of(v)
    q = jnp.round(v * factor).astype(I32)
    return join16(q, 0), jnp.broadcast_to(e.astype(I32), (8, v.shape[1]))


def low16(t):
    return (t << 16) >> 16


def high16(t):
    return t >> 16


def unscale(e):
    return jnp.exp2(e.astype(F32)) * (1.0 / TOP)


def decode_lanes(ref, rows):
    ex = ref[rows : rows + 1, :]
    q = ref[0:rows, :]
    low = low16(q).astype(F32) * unscale(low16(ex))
    high = high16(q).astype(F32) * unscale(high16(ex))
    return jnp.concatenate([low, high], axis=1)


def factor_block(w, blk):
    n = w.shape[0]
    o = blk * NB
    r8 = lax.broadcasted_iota(I32, (8, 128), 0)
    wb = w[o : o + NB, :]
    wide = wb.shape[1] // 128
    tile = lambda f: jnp.concatenate([f] * wide, axis=1)
    strips = [wb[8 * s : 8 * s + 8, :] for s in range(NB // 8)]
    for s in range(NB // 8):
        so = o + 8 * s
        left = NB // 8 - s
        cols = [
            [jnp.broadcast_to(strips[t][:, so + k : so + k + 1], (8, 128)) for k in range(8)]
            for t in range(s, NB // 8)
        ]
        st = strips[s]
        scale = jnp.zeros((8, 128), F32)
        fs = [[None] * 8 for _ in range(left)]
        for k in range(8):
            pivot = jnp.broadcast_to(cols[0][k][k : k + 1, :], (8, 128))
            inverse = 1.0 / pivot
            scale = jnp.where(r8 == k, lax.rsqrt(pivot), scale)
            for t in range(left):
                f = cols[t][k] * inverse
                fs[t][k] = jnp.where(r8 > k, f, 0.0) if t == 0 else f
            for j in range(k + 1, 8):
                u = jnp.broadcast_to(cols[0][j][k : k + 1, :], (8, 128))
                for t in range(left):
                    cols[t][j] = cols[t][j] - fs[t][k] * u
        for k in range(8):
            st = st - tile(fs[0][k]) * jnp.broadcast_to(st[k : k + 1, :], st.shape)
        for t in range(1, left):
            acc = strips[s + t]
            for k in range(8):
                acc = acc - tile(fs[t][k]) * jnp.broadcast_to(st[k : k + 1, :], st.shape)
            strips[s + t] = acc
        strips[s] = st
        w[so : so + 8, :] = st * tile(scale)
    if o + NB < n:
        y = w[o : o + NB, :]
        later = y[:, o + NB : n]
        w[o + NB : n, :] = w[o + NB : n, :] - lax.dot_general(
            later, y, (((0,), (0,)), ((), ())), precision=HI, preferred_element_type=F32
        )


def kernel(
    front_ref, omega_ref, psi_ref, length_ref, chosen_ref, assign_ref, pivot_ref,
    row_ref, col_ref,
    cbuf, ombuf, raw, psit, pivots, w, mt, psend, pown, precv, racc, sfin,
    xsend, xrecv, rq, rslot, rrecv, cq, cslot, crecv,
    csem, insem, om_send, om_recv, p_send, p_recv, x_send, x_recv, r_send, r_recv, c_send, c_recv,
):
    f = lax.axis_index("front")
    b = lax.axis_index("blk")
    X = b // 2
    c = lax.rem(b, 2)
    rows = 1024
    half = rows // 2
    blk_at = lambda dx, core: lax.rem(X + dx, 4) * 2 + core
    right = {"blk": blk_at(1, c)}
    left = {"blk": blk_at(3, c)}
    partner = {"blk": blk_at(0, 1 - c)}
    z, y = f // 4, lax.rem(f, 4)
    offs = [(dz, dy) for dz in range(4) for dy in range(4)][1:]
    front_at = lambda dz, dy: lax.rem(z + dz, 4) * 4 + lax.rem(y + dy, 4)

    barrier = pltpu.get_barrier_semaphore()
    peers = [right, left, partner] + [{"front": front_at(*o)} for o in offs]
    for peer in peers:
        pl.semaphore_signal(barrier, inc=1, device_id=peer, device_id_type=MESH)

    omega_in = pltpu.make_async_copy(omega_ref.at[0], raw.at[0], insem.at[0])
    psi_in = pltpu.make_async_copy(psi_ref.at[0], raw.at[1], insem.at[1])
    pivot_in = pltpu.make_async_copy(pivot_ref, pivots, insem.at[2])
    omega_in.start()
    psi_in.start()

    def chunk_in(dx, core):
        j = blk_at(dx, core)
        return pltpu.make_async_copy(
            front_ref.at[0, :, pl.ds(pl.multiple_of(j * rows, rows), rows)], cbuf.at[j], csem.at[j]
        )

    for k in range(4):
        chunk_in((k + 2) % 4, 1 - c).start()
        chunk_in((k + 2) % 4, c).start()
    pivot_in.start()

    length = length_ref[0]
    live = lax.broadcasted_iota(I32, (rows, 256), 0) + b * rows < length

    omega_in.wait()
    ombuf[b] = jnp.where(live, raw[0].astype(F32), 0.0).astype(BF16)
    pl.semaphore_wait(barrier, len(peers))

    def piece(blk, h, sem, to):
        ref = ombuf.at[blk, pl.ds(h * half, half)]
        return pltpu.make_async_remote_copy(
            src_ref=ref, dst_ref=ref, send_sem=om_send.at[sem], recv_sem=om_recv.at[sem],
            device_id=to, device_id_type=MESH,
        )

    own_right = [piece(b, h, h, right) for h in range(2)]
    own_left = [piece(b, h, 2 + h, left) for h in range(2)]
    own_right[0].start()
    own_left[1].start()
    own_right[1].start()
    own_left[0].start()
    cross = {}

    def cross_send(dx, h):
        cp = piece(blk_at(dx, c), h, 6 + dx * 2 + h, partner)
        cp.start()
        cross[dx, h] = cp

    cross_send(0, 0)
    cross_send(0, 1)

    psi_in.wait()
    psit[...] = jnp.where(live, raw[1].astype(F32), 0.0).T.astype(BF16)

    def partial_to_partner(dx):
        return pltpu.make_async_remote_copy(
            src_ref=psend.at[dx], dst_ref=precv.at[dx], send_sem=p_send.at[dx], recv_sem=p_recv.at[dx],
            device_id=partner, device_id_type=MESH,
        )

    @pl.loop(0, 4)
    def _(k):
        dx = lax.rem(k + 2, 4)
        chunk_in(dx, 1 - c).wait()
        psend[dx] = jnp.dot(psit[...], cbuf[blk_at(dx, 1 - c)], preferred_element_type=F32)
        partial_to_partner(dx).start()
        chunk_in(dx, c).wait()
        pown[dx] = jnp.dot(psit[...], cbuf[blk_at(dx, c)], preferred_element_type=F32)

    def row_add(dx, core, h, first=False):
        blk = blk_at(dx, core)
        t = jnp.dot(
            cbuf[blk, :, h * half : (h + 1) * half], ombuf[blk, h * half : (h + 1) * half, :],
            preferred_element_type=F32,
        )
        racc[...] = t if first else racc[...] + t

    row_add(0, c, 0, True)
    row_add(0, c, 1)
    for h in range(2):
        cross[0, h].wait_recv()
        row_add(0, 1 - c, h)

    own_right[0].wait_recv()
    fwd_right = piece(blk_at(3, c), 0, 4, right)
    fwd_right.start()
    cross_send(3, 0)
    own_left[1].wait_recv()
    fwd_left = piece(blk_at(1, c), 1, 5, left)
    fwd_left.start()
    cross_send(1, 1)

    pivot_in.wait()
    parent = assign_ref[f, 0]
    w[:, 0:256] = pivots[parent]
    eye = lax.broadcasted_iota(I32, (256, 256), 0) == lax.broadcasted_iota(I32, (256, 256), 1)
    w[:, 256:512] = jnp.where(eye, 1.0, 0.0)
    factor_block(w, 0)
    factor_block(w, 1)

    for dx, h in ((3, 0), (1, 1)):
        row_add(dx, c, h)
        cross[dx, h].wait_recv()
        row_add(dx, 1 - c, h)

    own_right[1].wait_recv()
    cross_send(3, 1)
    own_left[0].wait_recv()
    cross_send(1, 0)

    factor_block(w, 2)
    factor_block(w, 3)
    mt[...] = w[:, 256:512].T

    for dx, h in ((3, 1), (1, 0)):
        row_add(dx, c, h)
        cross[dx, h].wait_recv()
        row_add(dx, 1 - c, h)

    for dx in (2, 1, 3, 0):
        partial_to_partner(dx).wait_recv()
        pown[dx] = pown[dx] + precv[dx]

    def ring(sem, to):
        return pltpu.make_async_remote_copy(
            src_ref=xsend.at[sem], dst_ref=xrecv.at[sem], send_sem=x_send.at[sem], recv_sem=x_recv.at[sem],
            device_id=to, device_id_type=MESH,
        )

    def ring_put(sem, v):
        q, e = encode_lanes(v)
        xsend[sem, 0:128, :] = q
        xsend[sem, 128:136, :] = e

    ring_get = lambda sem: decode_lanes(xrecv.at[sem], 128)
    part = lambda dx, g, h: pown[dx, g * 128 : (g + 1) * 128, h * half : (h + 1) * half]
    R1, R2, R3, L1, L2, L3 = 0, 2, 4, 6, 8, 10
    for g in range(2):
        ring_put(R1 + g, part(2, g, 0))
        ring_put(L1 + g, part(2, g, 1))

    fwd_right.wait_recv()
    cross_send(2, 0)
    fwd_left.wait_recv()
    cross_send(2, 1)
    copies = {}

    def ring_send(sem, to):
        copies[sem] = ring(sem, to)
        copies[sem].start()

    for g in range(2):
        ring_send(R1 + g, right)
        ring_send(L1 + g, left)
    row_add(2, c, 0)
    row_add(2, c, 1)
    for h in range(2):
        cross[2, h].wait_recv()
        row_add(2, 1 - c, h)

    sub_live = lax.broadcasted_iota(I32, (128, 256), 0) + b * rows
    for k in range(8):
        s = jnp.where(sub_live + k * 128 < length, racc[k * 128 : (k + 1) * 128, :], 0.0)
        zk = jnp.dot(s, mt[...], precision=HI, preferred_element_type=F32)
        q, e = encode_lanes(zk)
        rq[k, 0:128, :] = q
        rq[k, 128:136, :] = e
    rq[8] = jnp.zeros(rq.shape[1:], I32)
    for g in range(2):
        cq[g, 8] = jnp.zeros(cq.shape[2:], I32)
    source = []
    for m in range(16):
        at = jnp.int32(8)
        for k in range(8):
            at = jnp.where(chosen_ref[0, k] == m, jnp.int32(k), at)
        source.append(at)
    for m in range(16):
        rslot[m] = rq[source[m]]
    rsends = []
    for i, o in enumerate(offs):
        cp = pltpu.make_async_remote_copy(
            src_ref=rslot.at[front_at(*o)], dst_ref=rrecv.at[f], send_sem=r_send.at[i], recv_sem=r_recv.at[i],
            device_id={"front": front_at(*o)}, device_id_type=MESH,
        )
        cp.start()
        rsends.append(cp)
    rrecv[f] = rslot[f]

    for g in range(2):
        ring_put(R3 + g, part(1, g, 1))
        ring_put(L3 + g, part(3, g, 0))

    for g in range(2):
        copies[R1 + g].wait_recv()
        ring_put(R2 + g, part(1, g, 0) + ring_get(R1 + g))
        ring_send(R2 + g, right)
        ring_send(R3 + g, right)
        copies[L1 + g].wait_recv()
        ring_put(L2 + g, part(3, g, 1) + ring_get(L1 + g))
        ring_send(L2 + g, left)
        ring_send(L3 + g, left)

    lane_live = lax.broadcasted_iota(I32, (128, half), 1) + b * rows
    csends = []
    for g in range(2):
        lo, hi = g * 128, (g + 1) * 128
        copies[L3 + g].wait_recv()
        copies[R2 + g].wait_recv()
        s = part(0, g, 0) + ring_get(L3 + g) + ring_get(R2 + g)
        sfin[lo:hi, 0:half] = jnp.where(lane_live < length, s, 0.0)
        copies[R3 + g].wait_recv()
        copies[L2 + g].wait_recv()
        s = part(0, g, 1) + ring_get(R3 + g) + ring_get(L2 + g)
        sfin[lo:hi, half:rows] = jnp.where(lane_live + half < length, s, 0.0)
        for k in range(8):
            zk = lax.dot_general(
                sfin[0:hi, k * 128 : (k + 1) * 128], mt[0:hi, lo:hi], (((0,), (0,)), ((), ())),
                precision=HI, preferred_element_type=F32,
            )
            q, e = encode_rows(zk)
            cq[g, k, 0:64, :] = q
            cq[g, k, 64:72, :] = e
        for m in range(16):
            cslot[g, m] = cq[g, source[m]]
        for i, o in enumerate(offs):
            cp = pltpu.make_async_remote_copy(
                src_ref=cslot.at[g, front_at(*o)], dst_ref=crecv.at[g, f],
                send_sem=c_send.at[g, i], recv_sem=c_recv.at[g, i],
                device_id={"front": front_at(*o)}, device_id_type=MESH,
            )
            cp.start()
            csends.append(cp)
        crecv[g, f] = cslot[g, f]

    weights = [[jnp.where(assign_ref[ch, 0] == p, 1.0, 0.0).astype(F32) for p in range(4)] for ch in range(16)]
    for cp in rsends:
        cp.wait_recv()

    @pl.loop(0, 4)
    def _(t):
        at = pl.ds(pl.multiple_of(t * 32, 32), 32)
        acc = [[jnp.zeros((32, 128), F32) for _ in range(2)] for _ in range(4)]
        for ch in range(16):
            q = rrecv[ch, at, :]
            ex = rrecv[ch, 128:129, :]
            for h, take in enumerate((low16, high16)):
                v = take(q).astype(F32)
                u = unscale(take(ex))
                for p in range(4):
                    acc[p][h] = acc[p][h] + v * (u * weights[ch][p])
        for p in range(4):
            row_ref[p, at, 0:128] = acc[p][0]
            row_ref[p, at, 128:256] = acc[p][1]

    for g in range(2):
        for cp in csends[g * 15 : (g + 1) * 15]:
            cp.wait_recv()

        @pl.loop(0, 2)
        def _(t):
            at = pl.ds(pl.multiple_of(t * 32, 32), 32)
            acc = [[jnp.zeros((32, 128), F32) for _ in range(2)] for _ in range(4)]
            for ch in range(16):
                q = crecv[g, ch, at, :]
                u = unscale(crecv[g, ch, 64:65, :])
                for h, take in enumerate((low16, high16)):
                    v = take(q).astype(F32)
                    for p in range(4):
                        acc[p][h] = acc[p][h] + v * (u * weights[ch][p])
            for p in range(4):
                for h in range(2):
                    rows_at = pl.ds(pl.multiple_of(h * 64 + t * 32, 32), 32)
                    col_ref[p, rows_at, g * 128 : (g + 1) * 128] = acc[p][h]

    for cp in own_right + own_left + [fwd_right, fwd_left] + list(cross.values()) + list(copies.values()):
        cp.wait_send()
    for dx in range(4):
        partial_to_partner(dx).wait_send()
    for cp in rsends + csends:
        cp.wait_send()


def on_device(contribution, omega_cols, psi_cols, lengths, selectors, assign, pivot_block):
    any_ref = pl.BlockSpec(memory_space=pl.ANY)
    smem = pl.BlockSpec(memory_space=pltpu.SMEM)
    vmem = pl.BlockSpec(memory_space=pltpu.VMEM)
    dma = pltpu.SemaphoreType.DMA
    row, col = pl.pallas_call(
        kernel,
        out_shape=[jax.ShapeDtypeStruct((4, 128, 256), F32)] * 2,
        in_specs=[any_ref, any_ref, any_ref, smem, smem, smem, any_ref],
        out_specs=[vmem, vmem],
        scratch_shapes=[
            pltpu.VMEM((8, 1024, 1024), BF16),
            pltpu.VMEM((8, 1024, 256), BF16),
            pltpu.VMEM((2, 1024, 256), BF16),
            pltpu.VMEM((256, 1024), BF16),
            pltpu.VMEM((4, 256, 256), F32),
            pltpu.VMEM((256, 512), F32),
            pltpu.VMEM((256, 256), F32),
            pltpu.VMEM((4, 256, 1024), F32),
            pltpu.VMEM((4, 256, 1024), F32),
            pltpu.VMEM((4, 256, 1024), F32),
            pltpu.VMEM((1024, 256), F32),
            pltpu.VMEM((256, 1024), F32),
            pltpu.VMEM((12, 136, 256), I32),
            pltpu.VMEM((12, 136, 256), I32),
            pltpu.VMEM((9, 136, 128), I32),
            pltpu.VMEM((16, 136, 128), I32),
            pltpu.VMEM((16, 136, 128), I32),
            pltpu.VMEM((2, 9, 72, 128), I32),
            pltpu.VMEM((2, 16, 72, 128), I32),
            pltpu.VMEM((2, 16, 72, 128), I32),
            dma((8,)),
            dma((3,)),
            dma((14,)),
            dma((14,)),
            dma((4,)),
            dma((4,)),
            dma((12,)),
            dma((12,)),
            dma((15,)),
            dma((15,)),
            dma((2, 15)),
            dma((2, 15)),
        ],
        compiler_params=pltpu.CompilerParams(
            collective_id=0, has_side_effects=True, vmem_limit_bytes=60 * 2**20
        ),
        cost_estimate=pl.CostEstimate(flops=9_000_000_000, bytes_accessed=20_000_000, transcendentals=0),
    )(contribution, omega_cols, psi_cols, lengths, selectors, assign, pivot_block)
    return (jnp.transpose(row, (1, 0, 2))[None], jnp.transpose(col, (1, 0, 2))[None])


def solution(mesh):
    in_specs = (
        P("front", "blk", None),
        P("front", "blk", None),
        P("front", "blk", None),
        P("front"),
        P("front", "blk"),
        P(),
        P(),
    )
    out_specs = (P("blk", "front", None, None), P("blk", "front", None, None))
    return jax.shard_map(
        on_device, mesh=mesh, in_specs=in_specs, out_specs=out_specs, check_vma=False
    )
```

```python
import functools

import jax
import jax.numpy as jnp
from jax import lax
from jax.experimental import pallas as pl
from jax.experimental.pallas import tpu as pltpu
from jax.sharding import PartitionSpec as P

MESH = pl.DeviceIdType.MESH
HI = lax.Precision.HIGHEST
F32 = jnp.float32
I32 = jnp.int32
BF16 = jnp.bfloat16
NB = 64
TOP = 32766.0


def join16(t, axis):
    half = t.shape[axis] // 2
    low = lax.slice_in_dim(t, 0, half, axis=axis)
    high = lax.slice_in_dim(t, half, 2 * half, axis=axis)
    return (high << 16) | (low & 0xFFFF)


def scale_of(v):
    m = jnp.max(jnp.abs(v), axis=0, keepdims=True)
    e = jnp.floor(jnp.log2(jnp.maximum(m, 2.0**-100))) + 1.0
    return e, jnp.exp2(-e) * TOP


def encode_lanes(v):
    e, factor = scale_of(v)
    q = jnp.round(v * factor).astype(I32)
    ex = join16(e.astype(I32), 1)
    return join16(q, 1), ex


def encode_rows(v):
    e, factor = scale_of(v)
    q = jnp.round(v * factor).astype(I32)
    return join16(q, 0), e.astype(I32)


def low16(t):
    return (t << 16) >> 16


def high16(t):
    return t >> 16


def unscale(e):
    return jnp.exp2(e.astype(F32)) * (1.0 / TOP)


def decode_lanes(ref, rows):
    ex = ref[rows : rows + 1, :]
    q = ref[0:rows, :]
    low = low16(q).astype(F32) * unscale(low16(ex))
    high = high16(q).astype(F32) * unscale(high16(ex))
    return jnp.concatenate([low, high], axis=1)


def split(t):
    high = t.astype(BF16)
    return high, (t - high.astype(F32)).astype(BF16)


def dot_split(s, m_high, m_low):
    high, low = split(s)
    dot = lambda p, q: jnp.dot(p, q, preferred_element_type=F32)
    return dot(high, m_high) + (dot(low, m_high) + dot(high, m_low))


def factor_block(w, blk):
    n = w.shape[0]
    o = blk * NB
    r8 = lax.broadcasted_iota(I32, (8, 128), 0)
    wb = w[o : o + NB, :]
    wide = wb.shape[1] // 128
    tile = lambda f: jnp.concatenate([f] * wide, axis=1)
    strips = [wb[8 * s : 8 * s + 8, :] for s in range(NB // 8)]
    for s in range(NB // 8):
        so = o + 8 * s
        left = NB // 8 - s
        cols = [
            [jnp.broadcast_to(strips[t][:, so + k : so + k + 1], (8, 128)) for k in range(8)]
            for t in range(s, NB // 8)
        ]
        st = strips[s]
        scale = jnp.zeros((8, 128), F32)
        fs = [[None] * 8 for _ in range(left)]
        for k in range(8):
            pivot = jnp.broadcast_to(cols[0][k][k : k + 1, :], (8, 128))
            inverse = 1.0 / pivot
            scale = jnp.where(r8 == k, lax.rsqrt(pivot), scale)
            for t in range(left):
                f = cols[t][k] * inverse
                fs[t][k] = jnp.where(r8 > k, f, 0.0) if t == 0 else f
            for j in range(k + 1, 8):
                u = jnp.broadcast_to(cols[0][j][k : k + 1, :], (8, 128))
                for t in range(left):
                    cols[t][j] = cols[t][j] - fs[t][k] * u
        for k in range(8):
            st = st - tile(fs[0][k]) * jnp.broadcast_to(st[k : k + 1, :], st.shape)
        for t in range(1, left):
            acc = strips[s + t]
            for k in range(8):
                acc = acc - tile(fs[t][k]) * jnp.broadcast_to(st[k : k + 1, :], st.shape)
            strips[s + t] = acc
        strips[s] = st
        w[so : so + 8, :] = st * tile(scale)
    if o + NB < n:
        y = w[o : o + NB, :]
        later = y[:, o + NB : n]
        w[o + NB : n, :] = w[o + NB : n, :] - lax.dot_general(
            later, y, (((0,), (0,)), ((), ())), precision=HI, preferred_element_type=F32
        )


def kernel(
    front_ref, omega_ref, psi_ref, length_ref, chosen_ref, assign_ref, pivot_ref,
    row_ref, col_ref,
    cbuf, ombuf, raw, psit, pivots, w, mt, psend, pown, precv, racc, sfin,
    xsend, xrecv, quant, slots, arrived,
    csem, insem, om_send, om_recv, p_send, p_recv, x_send, x_recv, s_send, s_recv,
):
    f = lax.axis_index("front")
    b = lax.axis_index("blk")
    X = b // 2
    c = lax.rem(b, 2)
    rows = 1024
    half = rows // 2
    blk_at = lambda dx, core: lax.rem(X + dx, 4) * 2 + core
    right = {"blk": blk_at(1, c)}
    left = {"blk": blk_at(3, c)}
    partner = {"blk": blk_at(0, 1 - c)}
    z, y = f // 4, lax.rem(f, 4)
    offs = [(dz, dy) for dz in range(4) for dy in range(4)][1:]
    front_at = lambda dz, dy: lax.rem(z + dz, 4) * 4 + lax.rem(y + dy, 4)

    barrier = pltpu.get_barrier_semaphore()
    peers = [right, left, partner] + [{"front": front_at(*o)} for o in offs]
    for peer in peers:
        pl.semaphore_signal(barrier, inc=1, device_id=peer, device_id_type=MESH)

    omega_in = pltpu.make_async_copy(omega_ref.at[0], raw.at[0], insem.at[0])
    psi_in = pltpu.make_async_copy(psi_ref.at[0], raw.at[1], insem.at[1])
    pivot_in = pltpu.make_async_copy(pivot_ref, pivots, insem.at[2])
    omega_in.start()
    psi_in.start()

    def chunk_in(dx, core):
        j = blk_at(dx, core)
        return pltpu.make_async_copy(
            front_ref.at[0, :, pl.ds(pl.multiple_of(j * rows, rows), rows)], cbuf.at[j], csem.at[j]
        )

    length = length_ref[0]
    live = lax.broadcasted_iota(I32, (rows, 128), 0) + b * rows < length

    omega_in.wait()
    for k in range(4):
        chunk_in((k + 2) % 4, 1 - c).start()
        chunk_in((k + 2) % 4, c).start()
    pivot_in.start()
    for g in range(2):
        ombuf[g, b] = jnp.where(live, raw[0, :, g * 128 : (g + 1) * 128].astype(F32), 0.0).astype(BF16)
    pl.semaphore_wait(barrier, len(peers))

    sent = []

    def piece(g, blk, h, sem, to):
        ref = ombuf.at[g, blk, pl.ds(h * half, half)]
        cp = pltpu.make_async_remote_copy(
            src_ref=ref, dst_ref=ref, send_sem=om_send.at[g, sem], recv_sem=om_recv.at[g, sem],
            device_id=to, device_id_type=MESH,
        )
        cp.start()
        sent.append(cp)
        return cp

    cross = {}

    def cross_send(g, dx, h):
        cross[g, dx, h] = piece(g, blk_at(dx, c), h, 6 + dx * 2 + h, partner)

    own = {}
    for h in range(2):
        own[0, 0, h] = piece(0, b, h, h, right)
        own[0, 1, 1 - h] = piece(0, b, 1 - h, 3 - h, left)
    for g in range(2):
        for h in range(2):
            cross_send(g, 0, h)

    psi_in.wait()
    live_all = lax.broadcasted_iota(I32, (rows, 256), 0) + b * rows < length
    psit[...] = jnp.where(live_all, raw[1].astype(F32), 0.0).T.astype(BF16)

    def partial_to_partner(dx):
        return pltpu.make_async_remote_copy(
            src_ref=psend.at[dx], dst_ref=precv.at[dx], send_sem=p_send.at[dx], recv_sem=p_recv.at[dx],
            device_id=partner, device_id_type=MESH,
        )

    @pl.loop(0, 4)
    def _(k):
        dx = lax.rem(k + 2, 4)
        chunk_in(dx, 1 - c).wait()
        psend[dx] = jnp.dot(psit[...], cbuf[blk_at(dx, 1 - c)], preferred_element_type=F32)
        partial_to_partner(dx).start()
        chunk_in(dx, c).wait()
        pown[dx] = jnp.dot(psit[...], cbuf[blk_at(dx, c)], preferred_element_type=F32)

    def row_add(g, dx, core, h, first=False):
        blk = blk_at(dx, core)
        t = jnp.dot(
            cbuf[blk, :, h * half : (h + 1) * half], ombuf[g, blk, h * half : (h + 1) * half, :],
            preferred_element_type=F32,
        )
        racc[g] = t if first else racc[g] + t

    def row_adds(g, pieces, first=False):
        @pl.loop(0, 2)
        def _(t):
            at = pl.ds(pl.multiple_of(t * 512, 512), 512)
            acc = None if first else racc[g, at, :]
            for dx, core, h in pieces:
                blk = blk_at(dx, core)
                v = jnp.dot(
                    cbuf[blk, at, h * half : (h + 1) * half], ombuf[g, blk, h * half : (h + 1) * half, :],
                    preferred_element_type=F32,
                )
                acc = v if acc is None else acc + v
            racc[g, at, :] = acc

    both = lambda pieces: [(dx, core, h) for dx, h in pieces for core in (c, 1 - c)]

    def row_add_own(g):
        for h in range(2):
            row_add(g, 0, c, h, h == 0)
            row_add(g, 0, 1 - c, h)

    def row_add_near(g, pieces):
        for dx, h in pieces:
            row_add(g, dx, c, h)
            row_add(g, dx, 1 - c, h)

    near_first, near_second = ((3, 0), (1, 1)), ((3, 1), (1, 0))

    own[1, 0, 0] = piece(1, b, 0, 0, right)
    own[1, 1, 1] = piece(1, b, 1, 3, left)
    passed = {}

    def pass_on(g):
        own[g, 0, 0].wait_recv()
        passed[g, 0] = piece(g, blk_at(3, c), 0, 4, right)
        cross_send(g, 3, 0)
        own[g, 1, 1].wait_recv()
        passed[g, 1] = piece(g, blk_at(1, c), 1, 5, left)
        cross_send(g, 1, 1)

    def cross_second(g):
        own[g, 0, 1].wait_recv()
        cross_send(g, 3, 1)
        own[g, 1, 0].wait_recv()
        cross_send(g, 1, 0)

    def cross_third(g):
        for h in range(2):
            passed[g, h].wait_recv()
            cross_send(g, 2, h)

    def wait_cross(g, pieces):
        for dx, h in pieces:
            cross[g, dx, h].wait_recv()

    pass_on(0)

    pivot_in.wait()
    parent = assign_ref[f]
    w[:, 0:256] = pivots[parent]
    eye = lax.broadcasted_iota(I32, (256, 256), 0) == lax.broadcasted_iota(I32, (256, 256), 1)
    w[:, 256:512] = jnp.where(eye, 1.0, 0.0)
    wait_cross(0, ((0, 0), (0, 1)))
    row_add_own(0)
    factor_block(w, 0)
    own[1, 0, 1] = piece(1, b, 1, 1, right)
    own[1, 1, 0] = piece(1, b, 0, 2, left)
    cross_second(0)
    wait_cross(0, near_first)
    row_add_near(0, near_first)
    factor_block(w, 1)

    def keep_inverse(g):
        m_high, m_low = split(w[g * 128 : (g + 1) * 128, 256:512].T)
        mt[0, :, g * 128 : (g + 1) * 128] = m_high
        mt[1, :, g * 128 : (g + 1) * 128] = m_low

    keep_inverse(0)

    for dx in (2, 1, 3, 0):
        partial_to_partner(dx).wait_recv()
        pown[dx] = pown[dx] + precv[dx]

    def ring_put(sem, v):
        q, e = encode_lanes(v)
        xsend[sem, 0:128, :] = q
        xsend[sem, 128:129, :] = e

    ring_get = lambda sem: decode_lanes(xrecv.at[sem], 128)
    copies = {}

    def ring_send(sem, to):
        copies[sem] = pltpu.make_async_remote_copy(
            src_ref=xsend.at[sem], dst_ref=xrecv.at[sem], send_sem=x_send.at[sem], recv_sem=x_recv.at[sem],
            device_id=to, device_id_type=MESH,
        )
        copies[sem].start()
        sent.append(copies[sem])

    part = lambda dx, g, h: pown[dx, g * 128 : (g + 1) * 128, h * half : (h + 1) * half]
    R1, R2, R3, L1, L2, L3 = 0, 2, 4, 6, 8, 10
    for g in range(2):
        ring_put(R1 + g, part(2, g, 0))
        ring_put(L1 + g, part(2, g, 1))
    for g in range(2):
        ring_put(R3 + g, part(1, g, 1))
        ring_put(L3 + g, part(3, g, 0))
    wait_cross(1, ((0, 0), (0, 1)))
    row_adds(1, both(((0, 0), (0, 1))), True)

    cross_third(0)
    pass_on(1)
    wait_cross(0, near_second)
    row_adds(0, both(near_second) + [(2, c, 0), (2, c, 1)])
    wait_cross(0, ((2, 0), (2, 1)))
    row_adds(0, [(2, 1 - c, 0), (2, 1 - c, 1)])

    for mat in range(2):
        for g in range(2):
            quant[mat, g, 8] = jnp.zeros(quant.shape[3:], I32)
    source = []
    for m in range(16):
        at = jnp.int32(8)
        for k in range(8):
            at = jnp.where(chosen_ref[0, k] == m, jnp.int32(k), at)
        source.append(at)
    placed = {}

    def place(mat, g):
        for m in range(16):
            slots[mat, g, m] = quant[mat, g, source[m]]
        placed[mat, g] = []
        for i, o in enumerate(offs):
            cp = pltpu.make_async_remote_copy(
                src_ref=slots.at[mat, g, front_at(*o)], dst_ref=arrived.at[mat, g, f],
                send_sem=s_send.at[mat, g, i], recv_sem=s_recv.at[mat, g, i],
                device_id={"front": front_at(*o)}, device_id_type=MESH,
            )
            cp.start()
            sent.append(cp)
            placed[mat, g].append(cp)
        arrived[mat, g, f] = slots[mat, g, f]

    def keep_quant(mat, g, k, zk):
        q, e = encode_rows(zk)
        quant[mat, g, k, 0:64, :] = q
        quant[mat, g, k, 64:65, :] = e

    sub_live = lax.broadcasted_iota(I32, (128, 128), 0) + b * rows

    def solve_rows(g):
        hi = (g + 1) * 128
        for k in range(8):
            parts = [racc[t, k * 128 : (k + 1) * 128, :] for t in range(g + 1)]
            s = jnp.concatenate([jnp.where(sub_live + k * 128 < length, t, 0.0) for t in parts], axis=1)
            keep_quant(0, g, k, dot_split(s, mt[0, 0:hi, hi - 128 : hi], mt[1, 0:hi, hi - 128 : hi]))
        place(0, g)

    solve_rows(0)

    ring_send(R1, right)
    ring_send(L1, left)
    cross_third(1)
    cross_second(1)
    wait_cross(1, near_first)
    wait_cross(1, near_second)
    row_add_near(1, near_first)
    row_add_near(1, near_second)
    factor_block(w, 2)
    ring_send(R1 + 1, right)
    ring_send(L1 + 1, left)
    wait_cross(1, ((2, 0), (2, 1)))
    for h in range(2):
        row_add(1, 2, c, h)
        row_add(1, 2, 1 - c, h)
    factor_block(w, 3)
    keep_inverse(1)

    def ring_middle(g):
        copies[R1 + g].wait_recv()
        ring_put(R2 + g, part(1, g, 0) + ring_get(R1 + g))
        ring_send(R2 + g, right)
        ring_send(R3 + g, right)
        copies[L1 + g].wait_recv()
        ring_put(L2 + g, part(3, g, 1) + ring_get(L1 + g))
        ring_send(L2 + g, left)
        ring_send(L3 + g, left)

    ring_middle(0)
    solve_rows(1)
    ring_middle(1)

    lane_live = lax.broadcasted_iota(I32, (128, half), 1) + b * rows

    def finish_columns(g):
        lo, hi = g * 128, (g + 1) * 128
        copies[L3 + g].wait_recv()
        copies[R2 + g].wait_recv()
        s = part(0, g, 0) + ring_get(L3 + g) + ring_get(R2 + g)
        sfin[lo:hi, 0:half] = jnp.where(lane_live < length, s, 0.0)
        copies[R3 + g].wait_recv()
        copies[L2 + g].wait_recv()
        s = part(0, g, 1) + ring_get(R3 + g) + ring_get(L2 + g)
        sfin[lo:hi, half:rows] = jnp.where(lane_live + half < length, s, 0.0)
        for k in range(8):
            s = sfin[0:hi, k * 128 : (k + 1) * 128].T
            keep_quant(1, g, k, dot_split(s, mt[0, 0:hi, lo:hi], mt[1, 0:hi, lo:hi]))
        place(1, g)

    weights = [[jnp.where(assign_ref[ch] == p, 1.0, 0.0).astype(F32) for p in range(4)] for ch in range(16)]

    def gather(mat, g):
        for cp in placed[mat, g]:
            cp.wait_recv()
        out = (row_ref, col_ref)[mat]

        @pl.loop(0, 2)
        def _(t):
            at = pl.ds(pl.multiple_of(t * 32, 32), 32)
            acc = [[jnp.zeros((32, 128), F32) for _ in range(2)] for _ in range(4)]
            for ch in range(16):
                q = arrived[mat, g, ch, at, :]
                u = unscale(arrived[mat, g, ch, 64:65, :])
                for h, take in enumerate((low16, high16)):
                    v = take(q).astype(F32)
                    for p in range(4):
                        acc[p][h] = acc[p][h] + v * (u * weights[ch][p])
            for p in range(4):
                for h in range(2):
                    out[pl.ds(h * 512 + t * 256 + g * 4 + p, 32, stride=8), :] = acc[p][h]

    gather(0, 0)
    finish_columns(0)
    gather(0, 1)
    finish_columns(1)
    gather(1, 0)
    gather(1, 1)

    for cp in sent:
        cp.wait_send()
    for dx in range(4):
        partial_to_partner(dx).wait_send()


def panel_of(t):
    return jnp.transpose(t.reshape(1, 128, 2, 4, 128), (0, 1, 3, 2, 4)).reshape(1, 128, 4, 256)


def on_device(contribution, omega_cols, psi_cols, lengths, selectors, assign, pivot_block):
    any_ref = pl.BlockSpec(memory_space=pl.ANY)
    smem = pl.BlockSpec(memory_space=pltpu.SMEM)
    vmem = pl.BlockSpec(memory_space=pltpu.VMEM)
    dma = pltpu.SemaphoreType.DMA
    row, col = pl.pallas_call(
        kernel,
        out_shape=[jax.ShapeDtypeStruct((1024, 128), F32)] * 2,
        in_specs=[any_ref, any_ref, any_ref, smem, smem, smem, any_ref],
        out_specs=[vmem, vmem],
        scratch_shapes=[
            pltpu.VMEM((8, 1024, 1024), BF16),
            pltpu.VMEM((2, 8, 1024, 128), BF16),
            pltpu.VMEM((2, 1024, 256), BF16),
            pltpu.VMEM((256, 1024), BF16),
            pltpu.VMEM((4, 256, 256), F32),
            pltpu.VMEM((256, 512), F32),
            pltpu.VMEM((2, 256, 256), BF16),
            pltpu.VMEM((4, 256, 1024), F32),
            pltpu.VMEM((4, 256, 1024), F32),
            pltpu.VMEM((4, 256, 1024), F32),
            pltpu.VMEM((2, 1024, 128), F32),
            pltpu.VMEM((256, 1024), F32),
            pltpu.VMEM((12, 129, 256), I32),
            pltpu.VMEM((12, 129, 256), I32),
            pltpu.VMEM((2, 2, 9, 65, 128), I32),
            pltpu.VMEM((2, 2, 16, 65, 128), I32),
            pltpu.VMEM((2, 2, 16, 65, 128), I32),
            dma((8,)),
            dma((3,)),
            dma((2, 14)),
            dma((2, 14)),
            dma((4,)),
            dma((4,)),
            dma((12,)),
            dma((12,)),
            dma((2, 2, 15)),
            dma((2, 2, 15)),
        ],
        compiler_params=pltpu.CompilerParams(
            collective_id=0, has_side_effects=True, vmem_limit_bytes=60 * 2**20
        ),
        cost_estimate=pl.CostEstimate(flops=9_000_000_000, bytes_accessed=20_000_000, transcendentals=0),
    )(contribution, omega_cols, psi_cols, lengths, selectors, assign.reshape(-1), pivot_block)
    row, col = (jnp.where(lengths[0] > 0, t, 0.0) for t in (row, col))
    return (panel_of(row), panel_of(col))


def solution(mesh):
    in_specs = (
        P("front", "blk", None),
        P("front", "blk", None),
        P("front", "blk", None),
        P("front"),
        P("front", "blk"),
        P(),
        P(),
    )
    out_specs = (P("blk", "front", None, None), P("blk", "front", None, None))
    return jax.shard_map(
        on_device, mesh=mesh, in_specs=in_specs, out_specs=out_specs, check_vma=False
    )
```

```python
import functools

import jax
import jax.numpy as jnp
from jax import lax
from jax.experimental import pallas as pl
from jax.experimental.pallas import tpu as pltpu
from jax.sharding import PartitionSpec as P

MESH = pl.DeviceIdType.MESH
HI = lax.Precision.HIGHEST
F32 = jnp.float32
I32 = jnp.int32
BF16 = jnp.bfloat16
NB = 64
TOP = 32766.0


def join16(t, axis):
    half = t.shape[axis] // 2
    low = lax.slice_in_dim(t, 0, half, axis=axis)
    high = lax.slice_in_dim(t, half, 2 * half, axis=axis)
    return (high << 16) | (low & 0xFFFF)


def scale_of(v):
    m = jnp.max(jnp.abs(v), axis=0, keepdims=True)
    e = jnp.floor(jnp.log2(jnp.maximum(m, 2.0**-100))) + 1.0
    return e, jnp.exp2(-e) * TOP


def encode_lanes(v):
    e, factor = scale_of(v)
    q = jnp.round(v * factor).astype(I32)
    ex = join16(e.astype(I32), 1)
    return join16(q, 1), ex


def encode_rows(v):
    e, factor = scale_of(v)
    q = jnp.round(v * factor).astype(I32)
    return join16(q, 0), e.astype(I32)


def low16(t):
    return (t << 16) >> 16


def high16(t):
    return t >> 16


def unscale(e):
    return jnp.exp2(e.astype(F32)) * (1.0 / TOP)


def decode_lanes(ref, rows):
    ex = ref[rows : rows + 1, :]
    q = ref[0:rows, :]
    low = low16(q).astype(F32) * unscale(low16(ex))
    high = high16(q).astype(F32) * unscale(high16(ex))
    return jnp.concatenate([low, high], axis=1)


def split(t):
    high = t.astype(BF16)
    return high, (t - high.astype(F32)).astype(BF16)


def dot_split(s, m_high, m_low):
    high, low = split(s)
    dot = lambda p, q: jnp.dot(p, q, preferred_element_type=F32)
    return dot(high, m_high) + (dot(low, m_high) + dot(high, m_low))


def factor_block(w, blk):
    n = w.shape[0]
    o = blk * NB
    r8 = lax.broadcasted_iota(I32, (8, 128), 0)
    wb = w[o : o + NB, :]
    wide = wb.shape[1] // 128
    tile = lambda f: jnp.concatenate([f] * wide, axis=1)
    strips = [wb[8 * s : 8 * s + 8, :] for s in range(NB // 8)]
    for s in range(NB // 8):
        so = o + 8 * s
        left = NB // 8 - s
        cols = [
            [jnp.broadcast_to(strips[t][:, so + k : so + k + 1], (8, 128)) for k in range(8)]
            for t in range(s, NB // 8)
        ]
        st = strips[s]
        scale = jnp.zeros((8, 128), F32)
        fs = [[None] * 8 for _ in range(left)]
        for k in range(8):
            pivot = jnp.broadcast_to(cols[0][k][k : k + 1, :], (8, 128))
            inverse = 1.0 / pivot
            scale = jnp.where(r8 == k, lax.rsqrt(pivot), scale)
            for t in range(left):
                f = cols[t][k] * inverse
                fs[t][k] = jnp.where(r8 > k, f, 0.0) if t == 0 else f
            for j in range(k + 1, 8):
                u = jnp.broadcast_to(cols[0][j][k : k + 1, :], (8, 128))
                for t in range(left):
                    cols[t][j] = cols[t][j] - fs[t][k] * u
        for k in range(8):
            st = st - tile(fs[0][k]) * jnp.broadcast_to(st[k : k + 1, :], st.shape)
        for t in range(1, left):
            acc = strips[s + t]
            for k in range(8):
                acc = acc - tile(fs[t][k]) * jnp.broadcast_to(st[k : k + 1, :], st.shape)
            strips[s + t] = acc
        strips[s] = st
        w[so : so + 8, :] = st * tile(scale)
    if o + NB < n:
        y = w[o : o + NB, :]
        later = y[:, o + NB : n]
        w[o + NB : n, :] = w[o + NB : n, :] - lax.dot_general(
            later, y, (((0,), (0,)), ((), ())), precision=HI, preferred_element_type=F32
        )


def kernel(
    front_ref, omega_ref, psi_ref, length_in, chosen_in, assign_in, pivot_ref,
    row_out, col_out,
    length_ref, chosen_ref, assign_ref, row_ref, col_ref, cbuf, ombuf, raw, psit, pivots, w, mt, psend, pown, precv, racc, sfin,
    xsend, xrecv, quant, slots, arrived,
    csem, insem, om_send, om_recv, p_send, p_recv, x_send, x_recv, s_send, s_recv,
):
    f = lax.axis_index("front")
    b = lax.axis_index("blk")
    X = b // 2
    c = lax.rem(b, 2)
    rows = 1024
    half = rows // 2
    blk_at = lambda dx, core: lax.rem(X + dx, 4) * 2 + core
    right = {"blk": blk_at(1, c)}
    left = {"blk": blk_at(3, c)}
    partner = {"blk": blk_at(0, 1 - c)}
    z, y = f // 4, lax.rem(f, 4)
    hops = lambda o: min(o[0], 4 - o[0]) + min(o[1], 4 - o[1])
    offs = sorted([(dz, dy) for dz in range(4) for dy in range(4)][1:], key=lambda o: -hops(o))
    front_at = lambda dz, dy: lax.rem(z + dz, 4) * 4 + lax.rem(y + dy, 4)

    barrier = pltpu.get_barrier_semaphore()
    peers = [right, left, partner] + [{"front": front_at(*o)} for o in offs]
    for peer in peers:
        pl.semaphore_signal(barrier, inc=1, device_id=peer, device_id_type=MESH)

    omega_in = pltpu.make_async_copy(omega_ref.at[0], raw.at[0], insem.at[0])
    psi_in = pltpu.make_async_copy(psi_ref.at[0], raw.at[1], insem.at[1])
    pivot_in = pltpu.make_async_copy(pivot_ref, pivots, insem.at[2])
    omega_in.start()
    scalars_in = [
        pltpu.make_async_copy(source, to, insem.at[5 + i])
        for i, (source, to) in enumerate(
            ((length_in, length_ref), (chosen_in, chosen_ref), (assign_in, assign_ref))
        )
    ]
    for cp in scalars_in:
        cp.start()
    psi_in.start()

    def chunk_in(dx, core):
        j = blk_at(dx, core)
        return pltpu.make_async_copy(
            front_ref.at[0, :, pl.ds(pl.multiple_of(j * rows, rows), rows)], cbuf.at[j], csem.at[j]
        )

    for cp in scalars_in:
        cp.wait()
    length = length_ref[0]
    live = lax.broadcasted_iota(I32, (rows, 128), 0) + b * rows < length

    omega_in.wait()
    for k in range(4):
        chunk_in((k + 2) % 4, 1 - c).start()
        chunk_in((k + 2) % 4, c).start()
    pivot_in.start()
    for g in range(2):
        ombuf[g, b] = jnp.where(live, raw[0, :, g * 128 : (g + 1) * 128].astype(F32), 0.0).astype(BF16)
    pl.semaphore_wait(barrier, len(peers))

    sent = []

    def piece(g, blk, h, sem, to):
        ref = ombuf.at[g, blk, pl.ds(h * half, half)]
        cp = pltpu.make_async_remote_copy(
            src_ref=ref, dst_ref=ref, send_sem=om_send.at[g, sem], recv_sem=om_recv.at[g, sem],
            device_id=to, device_id_type=MESH,
        )
        cp.start()
        sent.append(cp)
        return cp

    cross = {}

    def cross_send(g, dx, h):
        cross[g, dx, h] = piece(g, blk_at(dx, c), h, 6 + dx * 2 + h, partner)

    own, passed = {}, {}
    own[0, 0, 0] = piece(0, b, 0, 0, right)
    own[0, 1, 1] = piece(0, b, 1, 3, left)
    for g in range(2):
        for h in range(2):
            cross_send(g, 0, h)

    def own_second(g):
        own[g, 0, 1] = piece(g, b, 1, 1, right)
        own[g, 1, 0] = piece(g, b, 0, 2, left)

    def pass_on(g):
        own[g, 0, 0].wait_recv()
        passed[g, 0] = piece(g, blk_at(3, c), 0, 4, right)
        cross_send(g, 3, 0)
        own[g, 1, 1].wait_recv()
        passed[g, 1] = piece(g, blk_at(1, c), 1, 5, left)
        cross_send(g, 1, 1)

    psi_in.wait()
    live_all = lax.broadcasted_iota(I32, (rows, 256), 0) + b * rows < length
    psit[...] = jnp.where(live_all, raw[1].astype(F32), 0.0).T.astype(BF16)

    def partial_to_partner(dx):
        return pltpu.make_async_remote_copy(
            src_ref=psend.at[dx], dst_ref=precv.at[dx], send_sem=p_send.at[dx], recv_sem=p_recv.at[dx],
            device_id=partner, device_id_type=MESH,
        )

    def column_partials(k):
        dx = (k + 2) % 4
        chunk_in(dx, 1 - c).wait()
        psend[dx] = jnp.dot(psit[...], cbuf[blk_at(dx, 1 - c)], preferred_element_type=F32)
        partial_to_partner(dx).start()
        chunk_in(dx, c).wait()
        pown[dx] = jnp.dot(psit[...], cbuf[blk_at(dx, c)], preferred_element_type=F32)

    column_partials(0)
    column_partials(1)
    own_second(0)
    column_partials(2)
    pass_on(0)
    column_partials(3)

    def row_add(g, dx, core, h, first=False):
        blk = blk_at(dx, core)
        t = jnp.dot(
            cbuf[blk, :, h * half : (h + 1) * half], ombuf[g, blk, h * half : (h + 1) * half, :],
            preferred_element_type=F32,
        )
        racc[g] = t if first else racc[g] + t

    def row_adds(g, pieces, first=False):
        @pl.loop(0, 2)
        def _(t):
            at = pl.ds(pl.multiple_of(t * 512, 512), 512)
            acc = None if first else racc[g, at, :]
            for dx, core, h in pieces:
                blk = blk_at(dx, core)
                v = jnp.dot(
                    cbuf[blk, at, h * half : (h + 1) * half], ombuf[g, blk, h * half : (h + 1) * half, :],
                    preferred_element_type=F32,
                )
                acc = v if acc is None else acc + v
            racc[g, at, :] = acc

    both = lambda pieces: [(dx, core, h) for dx, h in pieces for core in (c, 1 - c)]

    def row_add_own(g):
        for h in range(2):
            row_add(g, 0, c, h, h == 0)
            row_add(g, 0, 1 - c, h)

    def row_add_near(g, pieces):
        for dx, h in pieces:
            row_add(g, dx, c, h)
            row_add(g, dx, 1 - c, h)

    near_first, near_second = ((3, 0), (1, 1)), ((3, 1), (1, 0))

    def cross_second(g):
        own[g, 0, 1].wait_recv()
        cross_send(g, 3, 1)
        own[g, 1, 0].wait_recv()
        cross_send(g, 1, 0)

    def cross_third(g):
        for h in range(2):
            passed[g, h].wait_recv()
            cross_send(g, 2, h)

    def wait_cross(g, pieces):
        for dx, h in pieces:
            cross[g, dx, h].wait_recv()

    pivot_in.wait()
    parent = assign_ref[f]
    w[:, 0:256] = pivots[parent]
    eye = lax.broadcasted_iota(I32, (256, 256), 0) == lax.broadcasted_iota(I32, (256, 256), 1)
    w[:, 256:512] = jnp.where(eye, 1.0, 0.0)
    wait_cross(0, ((0, 0), (0, 1)))
    row_add_own(0)
    factor_block(w, 0)
    own[1, 0, 0] = piece(1, b, 0, 0, right)
    own[1, 1, 1] = piece(1, b, 1, 3, left)
    cross_second(0)
    wait_cross(0, near_first)
    row_add_near(0, near_first)
    factor_block(w, 1)

    def keep_inverse(g):
        m_high, m_low = split(w[g * 128 : (g + 1) * 128, 256:512].T)
        mt[0, :, g * 128 : (g + 1) * 128] = m_high
        mt[1, :, g * 128 : (g + 1) * 128] = m_low

    keep_inverse(0)

    cross_third(0)
    own_second(1)
    for dx in (2, 1, 3, 0):
        partial_to_partner(dx).wait_recv()
        pown[dx] = pown[dx] + precv[dx]

    def ring_put(sem, v):
        q, e = encode_lanes(v)
        xsend[sem, 0:128, :] = q
        xsend[sem, 128:129, :] = e

    ring_get = lambda sem: decode_lanes(xrecv.at[sem], 128)
    copies = {}

    def ring_send(sem, to):
        copies[sem] = pltpu.make_async_remote_copy(
            src_ref=xsend.at[sem], dst_ref=xrecv.at[sem], send_sem=x_send.at[sem], recv_sem=x_recv.at[sem],
            device_id=to, device_id_type=MESH,
        )
        copies[sem].start()
        sent.append(copies[sem])

    part = lambda dx, g, h: pown[dx, g * 128 : (g + 1) * 128, h * half : (h + 1) * half]
    R1, R2, R3, L1, L2, L3 = 0, 2, 4, 6, 8, 10
    for g in range(2):
        ring_put(R1 + g, part(2, g, 0))
        ring_put(L1 + g, part(2, g, 1))
    for g in range(2):
        ring_put(R3 + g, part(1, g, 1))
        ring_put(L3 + g, part(3, g, 0))
    wait_cross(0, near_second)
    row_adds(0, both(near_second) + [(2, c, 0), (2, c, 1)])
    pass_on(1)
    wait_cross(0, ((2, 0), (2, 1)))
    row_adds(0, [(2, 1 - c, 0), (2, 1 - c, 1)])

    for mat in range(2):
        for g in range(2):
            quant[mat, g, 8] = jnp.zeros(quant.shape[3:], I32)
    source = []
    for m in range(16):
        at = jnp.int32(8)
        for k in range(8):
            at = jnp.where(chosen_ref[0, k] == m, jnp.int32(k), at)
        source.append(at)
    placed = {}

    def place(mat, g):
        for m in range(16):
            slots[mat, g, m] = quant[mat, g, source[m]]
        placed[mat, g] = []
        for i, o in enumerate(offs):
            cp = pltpu.make_async_remote_copy(
                src_ref=slots.at[mat, g, front_at(*o)], dst_ref=arrived.at[mat, g, f],
                send_sem=s_send.at[mat, g, i], recv_sem=s_recv.at[mat, g, i],
                device_id={"front": front_at(*o)}, device_id_type=MESH,
            )
            cp.start()
            sent.append(cp)
            placed[mat, g].append(cp)
        arrived[mat, g, f] = slots[mat, g, f]

    def keep_quant(mat, g, k, zk):
        q, e = encode_rows(zk)
        quant[mat, g, k, 0:64, :] = q
        quant[mat, g, k, 64:65, :] = e

    sub_live = lax.broadcasted_iota(I32, (128, 128), 0) + b * rows

    def solve_rows(g):
        hi = (g + 1) * 128
        for k in range(8):
            parts = [racc[t, k * 128 : (k + 1) * 128, :] for t in range(g + 1)]
            s = jnp.concatenate([jnp.where(sub_live + k * 128 < length, t, 0.0) for t in parts], axis=1)
            keep_quant(0, g, k, dot_split(s, mt[0, 0:hi, hi - 128 : hi], mt[1, 0:hi, hi - 128 : hi]))
        place(0, g)

    solve_rows(0)
    ring_send(R1, right)
    ring_send(L1, left)
    wait_cross(1, ((0, 0), (0, 1)))
    row_add_own(1)
    factor_block(w, 2)
    ring_send(R1 + 1, right)
    ring_send(L1 + 1, left)
    cross_second(1)
    wait_cross(1, near_first)
    row_add_near(1, near_first)
    factor_block(w, 3)
    keep_inverse(1)

    def ring_middle(g):
        copies[R1 + g].wait_recv()
        ring_put(R2 + g, part(1, g, 0) + ring_get(R1 + g))
        ring_send(R2 + g, right)
        ring_send(R3 + g, right)
        copies[L1 + g].wait_recv()
        ring_put(L2 + g, part(3, g, 1) + ring_get(L1 + g))
        ring_send(L2 + g, left)
        ring_send(L3 + g, left)

    ring_middle(0)
    cross_third(1)
    wait_cross(1, near_second)
    row_adds(1, both(near_second) + [(2, c, 0), (2, c, 1)])
    wait_cross(1, ((2, 0), (2, 1)))
    row_adds(1, [(2, 1 - c, 0), (2, 1 - c, 1)])
    solve_rows(1)
    ring_middle(1)

    lane_live = lax.broadcasted_iota(I32, (128, half), 1) + b * rows

    def finish_columns(g):
        lo, hi = g * 128, (g + 1) * 128
        copies[L3 + g].wait_recv()
        copies[R2 + g].wait_recv()
        s = part(0, g, 0) + ring_get(L3 + g) + ring_get(R2 + g)
        sfin[lo:hi, 0:half] = jnp.where(lane_live < length, s, 0.0)
        copies[R3 + g].wait_recv()
        copies[L2 + g].wait_recv()
        s = part(0, g, 1) + ring_get(R3 + g) + ring_get(L2 + g)
        sfin[lo:hi, half:rows] = jnp.where(lane_live + half < length, s, 0.0)
        for k in range(8):
            s = sfin[0:hi, k * 128 : (k + 1) * 128].T
            keep_quant(1, g, k, dot_split(s, mt[0, 0:hi, lo:hi], mt[1, 0:hi, lo:hi]))
        place(1, g)

    weights = [[jnp.where(assign_ref[ch] == p, 1.0, 0.0).astype(F32) for p in range(4)] for ch in range(16)]

    def gather(mat, g):
        for cp in placed[mat, g]:
            cp.wait_recv()
        out = (row_ref, col_ref)[mat]

        @pl.loop(0, 2)
        def _(t):
            at = pl.ds(pl.multiple_of(t * 32, 32), 32)
            acc = [[jnp.zeros((32, 128), F32) for _ in range(2)] for _ in range(4)]
            for ch in range(16):
                q = arrived[mat, g, ch, at, :]
                u = unscale(arrived[mat, g, ch, 64:65, :])
                for h, take in enumerate((low16, high16)):
                    v = take(q).astype(F32)
                    for p in range(4):
                        acc[p][h] = acc[p][h] + v * (u * weights[ch][p])
            for p in range(4):
                for h in range(2):
                    out[pl.ds(h * 512 + t * 256 + g * 4 + p, 32, stride=8), :] = acc[p][h]

    gather(0, 0)
    finish_columns(0)
    gather(0, 1)
    row_done = pltpu.make_async_copy(row_ref, row_out, insem.at[3])
    row_done.start()
    finish_columns(1)
    gather(1, 0)
    gather(1, 1)
    col_done = pltpu.make_async_copy(col_ref, col_out, insem.at[4])
    col_done.start()

    for cp in sent:
        cp.wait_send()
    for dx in range(4):
        partial_to_partner(dx).wait_send()
    row_done.wait()
    col_done.wait()


def panel_of(t):
    return jnp.transpose(t.reshape(1, 128, 2, 4, 128), (0, 1, 3, 2, 4)).reshape(1, 128, 4, 256)


def on_device(contribution, omega_cols, psi_cols, lengths, selectors, assign, pivot_block):
    any_ref = pl.BlockSpec(memory_space=pl.ANY)
    hbm = pl.BlockSpec(memory_space=pl.ANY)
    dma = pltpu.SemaphoreType.DMA
    row, col = pl.pallas_call(
        kernel,
        out_shape=[jax.ShapeDtypeStruct((1024, 128), F32)] * 2,
        in_specs=[hbm] * 7,
        out_specs=[any_ref, any_ref],
        scratch_shapes=[
            pltpu.SMEM((1,), I32),
            pltpu.SMEM((1, 8), I32),
            pltpu.SMEM((16,), I32),
            pltpu.VMEM((1024, 128), F32),
            pltpu.VMEM((1024, 128), F32),
            pltpu.VMEM((8, 1024, 1024), BF16),
            pltpu.VMEM((2, 8, 1024, 128), BF16),
            pltpu.VMEM((2, 1024, 256), BF16),
            pltpu.VMEM((256, 1024), BF16),
            pltpu.VMEM((4, 256, 256), F32),
            pltpu.VMEM((256, 512), F32),
            pltpu.VMEM((2, 256, 256), BF16),
            pltpu.VMEM((4, 256, 1024), F32),
            pltpu.VMEM((4, 256, 1024), F32),
            pltpu.VMEM((4, 256, 1024), F32),
            pltpu.VMEM((2, 1024, 128), F32),
            pltpu.VMEM((256, 1024), F32),
            pltpu.VMEM((12, 129, 256), I32),
            pltpu.VMEM((12, 129, 256), I32),
            pltpu.VMEM((2, 2, 9, 65, 128), I32),
            pltpu.VMEM((2, 2, 16, 65, 128), I32),
            pltpu.VMEM((2, 2, 16, 65, 128), I32),
            dma((8,)),
            dma((8,)),
            dma((2, 14)),
            dma((2, 14)),
            dma((4,)),
            dma((4,)),
            dma((12,)),
            dma((12,)),
            dma((2, 2, 15)),
            dma((2, 2, 15)),
        ],
        compiler_params=pltpu.CompilerParams(
            collective_id=0, has_side_effects=True, vmem_limit_bytes=60 * 2**20
        ),
        cost_estimate=pl.CostEstimate(flops=9_000_000_000, bytes_accessed=20_000_000, transcendentals=0),
    )(contribution, omega_cols, psi_cols, lengths, selectors, assign.reshape(-1), pivot_block)
    row, col = (jnp.where(lengths[0] > 0, t, 0.0) for t in (row, col))
    return (panel_of(row), panel_of(col))


def solution(mesh):
    in_specs = (
        P("front", "blk", None),
        P("front", "blk", None),
        P("front", "blk", None),
        P("front"),
        P("front", "blk"),
        P(),
        P(),
    )
    out_specs = (P("blk", "front", None, None), P("blk", "front", None, None))
    return jax.shard_map(
        on_device, mesh=mesh, in_specs=in_specs, out_specs=out_specs, check_vma=False
    )
```

```python
import functools

import jax
import jax.numpy as jnp
from jax import lax
from jax.experimental import pallas as pl
from jax.experimental.pallas import tpu as pltpu
from jax.sharding import PartitionSpec as P

MESH = pl.DeviceIdType.MESH
HI = lax.Precision.HIGHEST
F32 = jnp.float32
I32 = jnp.int32
BF16 = jnp.bfloat16
NB = 64
TOP = 32766.0


def join16(t, axis):
    half = t.shape[axis] // 2
    low = lax.slice_in_dim(t, 0, half, axis=axis)
    high = lax.slice_in_dim(t, half, 2 * half, axis=axis)
    return (high << 16) | (low & 0xFFFF)


def scale_of(v):
    m = jnp.max(jnp.abs(v), axis=0, keepdims=True)
    e = jnp.floor(jnp.log2(jnp.maximum(m, 2.0**-100))) + 1.0
    return e, jnp.exp2(-e) * TOP


def encode_lanes(v):
    e, factor = scale_of(v)
    q = jnp.round(v * factor).astype(I32)
    ex = join16(e.astype(I32), 1)
    return join16(q, 1), ex


def encode_rows(v):
    e, factor = scale_of(v)
    q = jnp.round(v * factor).astype(I32)
    return join16(q, 0), e.astype(I32)


def low16(t):
    return (t << 16) >> 16


def high16(t):
    return t >> 16


def unscale(e):
    return jnp.exp2(e.astype(F32)) * (1.0 / TOP)


def decode_lanes(ref, rows):
    ex = ref[rows : rows + 1, :]
    q = ref[0:rows, :]
    low = low16(q).astype(F32) * unscale(low16(ex))
    high = high16(q).astype(F32) * unscale(high16(ex))
    return jnp.concatenate([low, high], axis=1)


def split(t):
    high = t.astype(BF16)
    return high, (t - high.astype(F32)).astype(BF16)


def dot_split(s, m_high, m_low):
    high, low = split(s)
    dot = lambda p, q: jnp.dot(p, q, preferred_element_type=F32)
    return dot(high, m_high) + (dot(low, m_high) + dot(high, m_low))


def factor_block(w, blk):
    n = w.shape[0]
    o = blk * NB
    r8 = lax.broadcasted_iota(I32, (8, 128), 0)
    at = o // 128 * 128
    span = slice(at, at + 384)
    wb = w[o : o + NB, span]
    wide = wb.shape[1] // 128
    tile = lambda f: jnp.concatenate([f] * wide, axis=1)
    strips = [wb[8 * s : 8 * s + 8, :] for s in range(NB // 8)]
    for s in range(NB // 8):
        so = o + 8 * s
        sa = so - at
        left = NB // 8 - s
        cols = [
            [jnp.broadcast_to(strips[t][:, sa + k : sa + k + 1], (8, 128)) for k in range(8)]
            for t in range(s, NB // 8)
        ]
        st = strips[s]
        scale = jnp.zeros((8, 128), F32)
        fs = [[None] * 8 for _ in range(left)]
        for k in range(8):
            pivot = jnp.broadcast_to(cols[0][k][k : k + 1, :], (8, 128))
            inverse = 1.0 / pivot
            scale = jnp.where(r8 == k, lax.rsqrt(pivot), scale)
            for t in range(left):
                f = cols[t][k] * inverse
                fs[t][k] = jnp.where(r8 > k, f, 0.0) if t == 0 else f
            for j in range(k + 1, 8):
                u = jnp.broadcast_to(cols[0][j][k : k + 1, :], (8, 128))
                for t in range(left):
                    cols[t][j] = cols[t][j] - fs[t][k] * u
        for k in range(8):
            st = st - tile(fs[0][k]) * jnp.broadcast_to(st[k : k + 1, :], st.shape)
        for t in range(1, left):
            acc = strips[s + t]
            for k in range(8):
                acc = acc - tile(fs[t][k]) * jnp.broadcast_to(st[k : k + 1, :], st.shape)
            strips[s + t] = acc
        strips[s] = st
        w[so : so + 8, span] = st * tile(scale)
    if o + NB < n:
        y = w[o : o + NB, span]
        later = w[o : o + NB, o + NB : n]
        w[o + NB : n, span] = w[o + NB : n, span] - lax.dot_general(
            later, y, (((0,), (0,)), ((), ())), precision=HI, preferred_element_type=F32
        )


def kernel(
    front_ref, omega_ref, psi_ref, length_in, chosen_in, assign_in, pivot_ref,
    row_out, col_out,
    length_ref, chosen_ref, assign_ref, row_ref, col_ref, cbuf, ombuf, raw, psit, pivots, w, mt, psend, pown, precv, racc, sfin,
    xsend, xrecv, quant, slots, arrived,
    csem, insem, om_send, om_recv, p_send, p_recv, x_send, x_recv, s_send, s_recv,
):
    f = lax.axis_index("front")
    b = lax.axis_index("blk")
    X = b // 2
    c = lax.rem(b, 2)
    rows = 1024
    half = rows // 2
    blk_at = lambda dx, core: lax.rem(X + dx, 4) * 2 + core
    right = {"blk": blk_at(1, c)}
    left = {"blk": blk_at(3, c)}
    partner = {"blk": blk_at(0, 1 - c)}
    z, y = f // 4, lax.rem(f, 4)
    hops = lambda o: min(o[0], 4 - o[0]) + min(o[1], 4 - o[1])
    offs = sorted([(dz, dy) for dz in range(4) for dy in range(4)][1:], key=lambda o: -hops(o))
    front_at = lambda dz, dy: lax.rem(z + dz, 4) * 4 + lax.rem(y + dy, 4)

    barrier = pltpu.get_barrier_semaphore()
    peers = [right, left, partner] + [{"front": front_at(*o)} for o in offs]
    for peer in peers:
        pl.semaphore_signal(barrier, inc=1, device_id=peer, device_id_type=MESH)

    omega_in = pltpu.make_async_copy(omega_ref.at[0], raw.at[0], insem.at[0])
    psi_in = pltpu.make_async_copy(psi_ref.at[0], raw.at[1], insem.at[1])
    pivot_in = pltpu.make_async_copy(pivot_ref, pivots, insem.at[2])
    omega_in.start()
    scalars_in = [
        pltpu.make_async_copy(source, to, insem.at[5 + i])
        for i, (source, to) in enumerate(
            ((length_in, length_ref), (chosen_in, chosen_ref), (assign_in, assign_ref))
        )
    ]
    for cp in scalars_in:
        cp.start()
    psi_in.start()

    def chunk_in(dx, core):
        j = blk_at(dx, core)
        return pltpu.make_async_copy(
            front_ref.at[0, :, pl.ds(pl.multiple_of(j * rows, rows), rows)], cbuf.at[j], csem.at[j]
        )

    for cp in scalars_in:
        cp.wait()
    length = length_ref[0]
    live = lax.broadcasted_iota(I32, (rows, 128), 0) + b * rows < length

    omega_in.wait()
    for k in range(4):
        chunk_in((k + 2) % 4, 1 - c).start()
        chunk_in((k + 2) % 4, c).start()
    pivot_in.start()
    for g in range(2):
        ombuf[g, b] = jnp.where(live, raw[0, :, g * 128 : (g + 1) * 128].astype(F32), 0.0).astype(BF16)
    pl.semaphore_wait(barrier, len(peers))

    sent = []

    def piece(g, blk, h, sem, to):
        ref = ombuf.at[g, blk, pl.ds(h * half, half)]
        cp = pltpu.make_async_remote_copy(
            src_ref=ref, dst_ref=ref, send_sem=om_send.at[g, sem], recv_sem=om_recv.at[g, sem],
            device_id=to, device_id_type=MESH,
        )
        cp.start()
        sent.append(cp)
        return cp

    cross = {}

    def cross_send(g, dx, h):
        cross[g, dx, h] = piece(g, blk_at(dx, c), h, 6 + dx * 2 + h, partner)

    own, passed = {}, {}
    own[0, 0, 0] = piece(0, b, 0, 0, right)
    own[0, 1, 1] = piece(0, b, 1, 3, left)
    for g in range(2):
        for h in range(2):
            cross_send(g, 0, h)

    def own_second(g):
        own[g, 0, 1] = piece(g, b, 1, 1, right)
        own[g, 1, 0] = piece(g, b, 0, 2, left)

    def pass_on(g):
        own[g, 0, 0].wait_recv()
        passed[g, 0] = piece(g, blk_at(3, c), 0, 4, right)
        cross_send(g, 3, 0)
        own[g, 1, 1].wait_recv()
        passed[g, 1] = piece(g, blk_at(1, c), 1, 5, left)
        cross_send(g, 1, 1)

    psi_in.wait()
    live_all = lax.broadcasted_iota(I32, (rows, 256), 0) + b * rows < length
    psit[...] = jnp.where(live_all, raw[1].astype(F32), 0.0).T.astype(BF16)

    def partial_to_partner(dx):
        return pltpu.make_async_remote_copy(
            src_ref=psend.at[dx], dst_ref=precv.at[dx], send_sem=p_send.at[dx], recv_sem=p_recv.at[dx],
            device_id=partner, device_id_type=MESH,
        )

    def column_partials(k):
        dx = (k + 2) % 4
        chunk_in(dx, 1 - c).wait()
        psend[dx] = jnp.dot(psit[...], cbuf[blk_at(dx, 1 - c)], preferred_element_type=F32)
        partial_to_partner(dx).start()
        chunk_in(dx, c).wait()
        pown[dx] = jnp.dot(psit[...], cbuf[blk_at(dx, c)], preferred_element_type=F32)

    column_partials(0)
    column_partials(1)
    own_second(0)
    column_partials(2)
    pass_on(0)
    column_partials(3)

    def row_add(g, dx, core, h, first=False):
        blk = blk_at(dx, core)
        t = jnp.dot(
            cbuf[blk, :, h * half : (h + 1) * half], ombuf[g, blk, h * half : (h + 1) * half, :],
            preferred_element_type=F32,
        )
        racc[g] = t if first else racc[g] + t

    def row_adds(g, pieces, first=False):
        @pl.loop(0, 2)
        def _(t):
            at = pl.ds(pl.multiple_of(t * 512, 512), 512)
            acc = None if first else racc[g, at, :]
            for dx, core, h in pieces:
                blk = blk_at(dx, core)
                v = jnp.dot(
                    cbuf[blk, at, h * half : (h + 1) * half], ombuf[g, blk, h * half : (h + 1) * half, :],
                    preferred_element_type=F32,
                )
                acc = v if acc is None else acc + v
            racc[g, at, :] = acc

    both = lambda pieces: [(dx, core, h) for dx, h in pieces for core in (c, 1 - c)]

    def row_add_own(g):
        for h in range(2):
            row_add(g, 0, c, h, h == 0)
            row_add(g, 0, 1 - c, h)

    def row_add_near(g, pieces):
        for dx, h in pieces:
            row_add(g, dx, c, h)
            row_add(g, dx, 1 - c, h)

    near_first, near_second = ((3, 0), (1, 1)), ((3, 1), (1, 0))

    def cross_second(g):
        own[g, 0, 1].wait_recv()
        cross_send(g, 3, 1)
        own[g, 1, 0].wait_recv()
        cross_send(g, 1, 0)

    def cross_third(g):
        for h in range(2):
            passed[g, h].wait_recv()
            cross_send(g, 2, h)

    def wait_cross(g, pieces):
        for dx, h in pieces:
            cross[g, dx, h].wait_recv()

    pivot_in.wait()
    parent = assign_ref[f]
    w[:, 0:256] = pivots[parent]
    eye = lax.broadcasted_iota(I32, (256, 256), 0) == lax.broadcasted_iota(I32, (256, 256), 1)
    w[:, 256:512] = jnp.where(eye, 1.0, 0.0)
    wait_cross(0, ((0, 0), (0, 1)))
    row_add_own(0)
    factor_block(w, 0)
    own[1, 0, 0] = piece(1, b, 0, 0, right)
    own[1, 1, 1] = piece(1, b, 1, 3, left)
    cross_second(0)
    wait_cross(0, near_first)
    row_add_near(0, near_first)
    factor_block(w, 1)

    def keep_inverse(g):
        m_high, m_low = split(w[g * 128 : (g + 1) * 128, 256:512].T)
        mt[0, :, g * 128 : (g + 1) * 128] = m_high
        mt[1, :, g * 128 : (g + 1) * 128] = m_low

    keep_inverse(0)

    cross_third(0)
    own_second(1)
    for dx in (2, 1, 3, 0):
        partial_to_partner(dx).wait_recv()
        pown[dx] = pown[dx] + precv[dx]

    def ring_put(sem, v):
        q, e = encode_lanes(v)
        xsend[sem, 0:128, :] = q
        xsend[sem, 128:129, :] = e

    ring_get = lambda sem: decode_lanes(xrecv.at[sem], 128)
    copies = {}

    def ring_send(sem, to):
        copies[sem] = pltpu.make_async_remote_copy(
            src_ref=xsend.at[sem], dst_ref=xrecv.at[sem], send_sem=x_send.at[sem], recv_sem=x_recv.at[sem],
            device_id=to, device_id_type=MESH,
        )
        copies[sem].start()
        sent.append(copies[sem])

    part = lambda dx, g, h: pown[dx, g * 128 : (g + 1) * 128, h * half : (h + 1) * half]
    R1, R2, R3, L1, L2, L3 = 0, 2, 4, 6, 8, 10
    for g in range(2):
        ring_put(R1 + g, part(2, g, 0))
        ring_put(L1 + g, part(2, g, 1))
    for g in range(2):
        ring_put(R3 + g, part(1, g, 1))
        ring_put(L3 + g, part(3, g, 0))
    wait_cross(0, near_second)
    row_adds(0, both(near_second) + [(2, c, 0), (2, c, 1)])
    pass_on(1)
    wait_cross(0, ((2, 0), (2, 1)))
    row_adds(0, [(2, 1 - c, 0), (2, 1 - c, 1)])

    for mat in range(2):
        for g in range(2):
            quant[mat, g, 8] = jnp.zeros(quant.shape[3:], I32)
    source = []
    for m in range(16):
        at = jnp.int32(8)
        for k in range(8):
            at = jnp.where(chosen_ref[0, k] == m, jnp.int32(k), at)
        source.append(at)
    placed = {}

    def place(mat, g):
        for m in range(16):
            slots[mat, g, m] = quant[mat, g, source[m]]
        placed[mat, g] = []
        for i, o in enumerate(offs):
            cp = pltpu.make_async_remote_copy(
                src_ref=slots.at[mat, g, front_at(*o)], dst_ref=arrived.at[mat, g, f],
                send_sem=s_send.at[mat, g, i], recv_sem=s_recv.at[mat, g, i],
                device_id={"front": front_at(*o)}, device_id_type=MESH,
            )
            cp.start()
            sent.append(cp)
            placed[mat, g].append(cp)
        arrived[mat, g, f] = slots[mat, g, f]

    def keep_quant(mat, g, k, zk):
        q, e = encode_rows(zk)
        quant[mat, g, k, 0:64, :] = q
        quant[mat, g, k, 64:65, :] = e

    sub_live = lax.broadcasted_iota(I32, (128, 128), 0) + b * rows

    def solve_rows(g):
        hi = (g + 1) * 128
        for k in range(8):
            parts = [racc[t, k * 128 : (k + 1) * 128, :] for t in range(g + 1)]
            s = jnp.concatenate([jnp.where(sub_live + k * 128 < length, t, 0.0) for t in parts], axis=1)
            keep_quant(0, g, k, dot_split(s, mt[0, 0:hi, hi - 128 : hi], mt[1, 0:hi, hi - 128 : hi]))
        place(0, g)

    solve_rows(0)
    ring_send(R1, right)
    ring_send(L1, left)
    wait_cross(1, ((0, 0), (0, 1)))
    row_add_own(1)
    factor_block(w, 2)
    ring_send(R1 + 1, right)
    ring_send(L1 + 1, left)
    cross_second(1)
    wait_cross(1, near_first)
    row_add_near(1, near_first)
    factor_block(w, 3)
    keep_inverse(1)

    def ring_middle(g):
        copies[R1 + g].wait_recv()
        ring_put(R2 + g, part(1, g, 0) + ring_get(R1 + g))
        ring_send(R2 + g, right)
        ring_send(R3 + g, right)
        copies[L1 + g].wait_recv()
        ring_put(L2 + g, part(3, g, 1) + ring_get(L1 + g))
        ring_send(L2 + g, left)
        ring_send(L3 + g, left)

    cross_third(1)
    ring_middle(0)
    wait_cross(1, near_second)
    row_adds(1, both(near_second) + [(2, c, 0), (2, c, 1)])
    wait_cross(1, ((2, 0), (2, 1)))
    row_adds(1, [(2, 1 - c, 0), (2, 1 - c, 1)])
    solve_rows(1)
    ring_middle(1)

    lane_live = lax.broadcasted_iota(I32, (128, half), 1) + b * rows

    def finish_columns(g):
        lo, hi = g * 128, (g + 1) * 128
        copies[L3 + g].wait_recv()
        copies[R2 + g].wait_recv()
        s = part(0, g, 0) + ring_get(L3 + g) + ring_get(R2 + g)
        sfin[lo:hi, 0:half] = jnp.where(lane_live < length, s, 0.0)
        copies[R3 + g].wait_recv()
        copies[L2 + g].wait_recv()
        s = part(0, g, 1) + ring_get(R3 + g) + ring_get(L2 + g)
        sfin[lo:hi, half:rows] = jnp.where(lane_live + half < length, s, 0.0)
        for k in range(8):
            s = sfin[0:hi, k * 128 : (k + 1) * 128].T
            keep_quant(1, g, k, dot_split(s, mt[0, 0:hi, lo:hi], mt[1, 0:hi, lo:hi]))
        place(1, g)

    weights = [[jnp.where(assign_ref[ch] == p, 1.0, 0.0).astype(F32) for p in range(4)] for ch in range(16)]

    def gather(mat, g, after=None):
        for cp in placed[mat, g]:
            cp.wait_recv()
        out = (row_ref, col_ref)[mat]

        def add_tile(t):
            at = pl.ds(t * 32 if after else pl.multiple_of(t * 32, 32), 32)
            acc = [[jnp.zeros((32, 128), F32) for _ in range(2)] for _ in range(4)]
            for ch in range(16):
                q = arrived[mat, g, ch, at, :]
                u = unscale(arrived[mat, g, ch, 64:65, :])
                for h, take in enumerate((low16, high16)):
                    v = take(q).astype(F32)
                    for p in range(4):
                        acc[p][h] = acc[p][h] + v * (u * weights[ch][p])
            for p in range(4):
                for h in range(2):
                    out[pl.ds(h * 512 + t * 256 + g * 4 + p, 32, stride=8), :] = acc[p][h]

        if after is None:
            pl.loop(0, 2)(add_tile)
        else:
            for t in range(2):
                add_tile(t)
                after(t)

    gather(0, 0)
    finish_columns(0)
    gather(0, 1)
    row_done = pltpu.make_async_copy(row_ref, row_out, insem.at[3])
    row_done.start()
    finish_columns(1)
    gather(1, 0)
    col_done = []

    def send_columns(t):
        for h in range(2):
            at = pl.ds(h * 512 + t * 256, 256)
            cp = pltpu.make_async_copy(col_ref.at[at], col_out.at[at], insem.at[8 + t * 2 + h])
            cp.start()
            col_done.append(cp)

    gather(1, 1, send_columns)

    for cp in sent:
        cp.wait_send()
    for dx in range(4):
        partial_to_partner(dx).wait_send()
    row_done.wait()
    for cp in col_done:
        cp.wait()


def panel_of(t):
    return jnp.transpose(t.reshape(1, 128, 2, 4, 128), (0, 1, 3, 2, 4)).reshape(1, 128, 4, 256)


def on_device(contribution, omega_cols, psi_cols, lengths, selectors, assign, pivot_block):
    any_ref = pl.BlockSpec(memory_space=pl.ANY)
    hbm = pl.BlockSpec(memory_space=pl.ANY)
    dma = pltpu.SemaphoreType.DMA
    row, col = pl.pallas_call(
        kernel,
        out_shape=[jax.ShapeDtypeStruct((1024, 128), F32)] * 2,
        in_specs=[hbm] * 7,
        out_specs=[any_ref, any_ref],
        scratch_shapes=[
            pltpu.SMEM((1,), I32),
            pltpu.SMEM((1, 8), I32),
            pltpu.SMEM((16,), I32),
            pltpu.VMEM((1024, 128), F32),
            pltpu.VMEM((1024, 128), F32),
            pltpu.VMEM((8, 1024, 1024), BF16),
            pltpu.VMEM((2, 8, 1024, 128), BF16),
            pltpu.VMEM((2, 1024, 256), BF16),
            pltpu.VMEM((256, 1024), BF16),
            pltpu.VMEM((4, 256, 256), F32),
            pltpu.VMEM((256, 512), F32),
            pltpu.VMEM((2, 256, 256), BF16),
            pltpu.VMEM((4, 256, 1024), F32),
            pltpu.VMEM((4, 256, 1024), F32),
            pltpu.VMEM((4, 256, 1024), F32),
            pltpu.VMEM((2, 1024, 128), F32),
            pltpu.VMEM((256, 1024), F32),
            pltpu.VMEM((12, 129, 256), I32),
            pltpu.VMEM((12, 129, 256), I32),
            pltpu.VMEM((2, 2, 9, 65, 128), I32),
            pltpu.VMEM((2, 2, 16, 65, 128), I32),
            pltpu.VMEM((2, 2, 16, 65, 128), I32),
            dma((8,)),
            dma((12,)),
            dma((2, 14)),
            dma((2, 14)),
            dma((4,)),
            dma((4,)),
            dma((12,)),
            dma((12,)),
            dma((2, 2, 15)),
            dma((2, 2, 15)),
        ],
        compiler_params=pltpu.CompilerParams(
            collective_id=0, has_side_effects=True, vmem_limit_bytes=60 * 2**20
        ),
        cost_estimate=pl.CostEstimate(flops=9_000_000_000, bytes_accessed=20_000_000, transcendentals=0),
    )(contribution, omega_cols, psi_cols, lengths, selectors, assign.reshape(-1), pivot_block)
    row, col = (jnp.where(lengths[0] > 0, t, 0.0) for t in (row, col))
    return (panel_of(row), panel_of(col))


def solution(mesh):
    in_specs = (
        P("front", "blk", None),
        P("front", "blk", None),
        P("front", "blk", None),
        P("front"),
        P("front", "blk"),
        P(),
        P(),
    )
    out_specs = (P("blk", "front", None, None), P("blk", "front", None, None))
    return jax.shard_map(
        on_device, mesh=mesh, in_specs=in_specs, out_specs=out_specs, check_vma=False
    )
```
